512 devices in a mesh: dp: 16 (over z_hi, x, core), fsdp: 32 (over y, z_lo).
Axes of the slice: x: 4, y: 4, z: 16 (z_hi: 2, z_lo: 8; z = z_hi * 8 + z_lo), core: 2. Of those that a mesh axis runs over, the one named last changes fastest.
Arguments:
- tokens: bfloat16 [65536, 8192], P(('dp', 'fsdp')), may hold values from -6 to 6
- norm_gain: bfloat16 [8192], replicated, may hold values from 0.25 to 1.75
- value_weight: bfloat16 [8192, 512], P('fsdp'), may hold values from -0.0625 to 0.0625
- input_basis: bfloat16 [8192, 64], P('fsdp'), may hold values from -0.0625 to 0.0625
- output_basis: bfloat16 [512, 64], replicated, may hold values from -0.25 to 0.25
- rotated_queries: bfloat16 [65536, 4096], P(('dp', 'fsdp')), may hold values from -150 to 150
- rotated_keys: bfloat16 [65536, 512], P(('dp', 'fsdp')), may hold values from -6 to 6
- upstream_grad: bfloat16 [65536, 4096], P(('dp', 'fsdp')), may hold values from -6 to 6
- example_lengths: int32 [512, 8], P(('dp', 'fsdp')), may hold values from 1 to 64, 128 in all within a row
- query_grads: bfloat16 [1024, 4096], P(('dp', 'fsdp')), may hold values from -0.0234375 to 0.0234375
Outputs:
- key_grad: bfloat16 [65536, 512], P(('dp', 'fsdp'))
- influence: float32 [4096, 1024], P(('dp', 'fsdp'))
The draws below stay inside these ranges and needn't reach their ends.
Inputs may be any that keep to these rules, and one draw needn't show every extreme that they name: `example_lengths`: each row sums to 128; its largest entry is 64.
All inputs are finite; a program needn't handle non-finite values.
Results may differ from the reference program's by a relative error of at most 0.014.
Values may be sent and summed in bfloat16 or wider, within the bound.
No kernel may reach another device: no remote copies, remote signals or barrier semaphores. Data moves between devices by JAX's collectives and lax.ppermute only.
A program may use at most 64 MiB of HBM per device.

```python
import math
import jax
import jax.numpy as jnp
import numpy as np
from jax import lax

D = 8192
HD = 128
GROUP = 8
KVH = 4
RANK = 64
TOK_DEV = 128
EX_DEV = 8
PROJ = 4096
TOKENS = 65536
QUERIES = 1024
N_DP = 16
N_FSDP = 32


def shared_keys(key):
    base = jax.random.truncated_normal(key, -6.0, 6.0, (TOKENS, KVH, HD), jnp.float32)
    places = jnp.arange(TOKENS) % 29 == 2
    blended = base
    return jnp.clip(jnp.where(places[:, None, None], blended, base), -6.0, 6.0)


def draw_rotated_keys(key, part):
    shared = shared_keys(key)
    return shared.reshape(TOKENS, KVH * HD).astype(jnp.bfloat16)


def draw_rotated_queries(key, part):
    key = jax.random.fold_in(key, 5)
    fresh = jax.random.truncated_normal(key, -6.0, 6.0, (TOKENS, KVH, GROUP, HD), jnp.float32)
    return fresh.reshape(TOKENS, KVH * GROUP * HD).astype(jnp.bfloat16)


def block_levels(own_key, extent, pieces, smallest, top_value):
    gain, own = 1.0, jax.random.fold_in(own_key, 6)
    for axis_at, blocks in pieces:
        heights = jnp.exp(jax.random.uniform(jax.random.fold_in(own, axis_at), (blocks,), jnp.float32, smallest / len(pieces), top_value / len(pieces)))
        gain = gain * jnp.repeat(heights, extent[axis_at] // blocks).reshape([-1 if axis == axis_at else 1 for axis in range(len(extent))])
    return gain


def profile(number_of, total, bound, skew):
    portions = [(1 << 20) // math.isqrt(grade ** skew) + 1 for grade in range(2, number_of + 1)]
    rest, holding = total - bound - (number_of - 1), [1] * (number_of - 1)
    while rest > 0:
        candidates = [i for i in range(number_of - 1) if holding[i] < bound]
        whole, left = sum([portions[i] for i in candidates]), rest
        for i in candidates:
            extra = min(bound - holding[i], max(1, left * portions[i] // whole), rest)
            holding[i] = holding[i] + extra
            rest = rest - extra
    return np.array([bound] + holding)


def uneven_parts(own_key, amount, total, most, lean):
    if amount == 2:
        one = jax.random.randint(own_key, (), max(1, total - most), min(most, total - 1) + 1)
        return jnp.stack([one, total - one])
    sizes = jnp.asarray(profile(amount, total, most, lean), jnp.int32)
    pairs = (amount - 1) // 2
    source_of, taker = sizes[1:1 + 2 * pairs:2], sizes[2:2 + 2 * pairs:2]
    margin = jnp.minimum(source_of - 1, most - taker)
    passed = jax.random.randint(jax.random.fold_in(own_key, 1), (pairs,), 0, 1 << 20) % (margin + 1)
    sizes = sizes.at[1:1 + 2 * pairs:2].set(source_of - passed).at[2:2 + 2 * pairs:2].set(taker + passed)
    return sizes[jax.random.permutation(jax.random.fold_in(own_key, 2), amount)]


def bell_draw(stream_key, dims, spread, reach, cuts=(), kind=jnp.bfloat16):
    values = spread * jax.random.normal(stream_key, dims, jnp.float32)
    if cuts:
        values = values * block_levels(stream_key, dims, cuts, -0.22, 0.18)
    return jnp.clip(values, -reach, reach).astype(kind)


def setup_inputs(seed: int = 0) -> dict:
    seeds = jax.random.split(jax.random.key(seed), 11)
    tokens = bell_draw(seeds[0], (TOKENS, D), 1.0, 6.0, ((0, 512),))
    norm_gain = jnp.clip(1.0 + 0.15 * jax.random.normal(seeds[1], (D,), jnp.float32), 0.25, 1.75).astype(jnp.bfloat16)
    value_weight = bell_draw(seeds[2], (D, KVH * HD), D ** -0.5, 0.0625, ((0, 32),))
    input_basis = bell_draw(seeds[3], (D, RANK), D ** -0.5, 0.0625, ((0, 32),))
    output_basis = bell_draw(seeds[4], (KVH * HD, RANK), (KVH * HD) ** -0.5, 0.25)
    rotated_queries = draw_rotated_queries(jax.random.fold_in(seeds[10], 71), 0)
    rotated_keys = draw_rotated_keys(jax.random.fold_in(seeds[10], 71), 0)
    upstream_grad = bell_draw(seeds[7], (TOKENS, KVH * GROUP * HD), 1.0, 6.0, ((0, 512),))
    example_lengths = jax.vmap(lambda own: uneven_parts(own, EX_DEV, TOK_DEV, TOK_DEV // 2, 1))(jax.random.split(seeds[8], (N_DP * N_FSDP))).reshape((N_DP * N_FSDP, EX_DEV)).astype(jnp.int32)
    query_grads = bell_draw(seeds[9], (QUERIES, PROJ), (0.25 / RANK), 0.0234375, ((0, 512),))
    return dict(tokens=tokens, norm_gain=norm_gain, value_weight=value_weight, input_basis=input_basis, output_basis=output_basis, rotated_queries=rotated_queries, rotated_keys=rotated_keys, upstream_grad=upstream_grad, example_lengths=example_lengths, query_grads=query_grads)


def attend(queries, keys, values, upstream, lengths):
    count = queries.shape[0]
    query_heads = queries.astype(jnp.float32).reshape(count, KVH, GROUP, HD)
    key_heads = keys.astype(jnp.float32).reshape(count, KVH, HD)
    value_heads = values.astype(jnp.float32).reshape(count, KVH, HD)
    grad_heads = upstream.astype(jnp.float32).reshape(count, KVH, GROUP, HD)
    bounds = jnp.cumsum(lengths).astype(jnp.int32)
    places = jnp.arange(count, dtype=jnp.int32)
    segment = lax.optimization_barrier(jnp.sum((places[:, None] >= bounds[None, :]).astype(jnp.int32), axis=1))
    allowed = (segment[:, None] == segment[None, :]) & (places[None, :] <= places[:, None])
    scale = 1.0 / math.sqrt(HD)
    logits = jnp.einsum('tjgd,ujd->jgtu', query_heads, key_heads) * scale
    logits = jnp.where(allowed, logits, jnp.float32(-1e+30))
    row_max = lax.optimization_barrier(jnp.max(logits, axis=-1, keepdims=True))
    expo = jnp.exp(logits - row_max)
    probs = expo / lax.optimization_barrier(jnp.sum(expo, axis=-1, keepdims=True))
    probs_low = probs.astype(jnp.bfloat16).astype(jnp.float32)
    value_grad = jnp.einsum('jgtu,tjgd->ujd', probs_low, grad_heads).astype(jnp.bfloat16)
    prob_grad = jnp.einsum('tjgd,ujd->jgtu', grad_heads, value_heads)
    logit_grad = probs * (prob_grad - lax.optimization_barrier(jnp.sum(probs * prob_grad, axis=-1, keepdims=True)))
    logit_low = logit_grad.astype(jnp.bfloat16).astype(jnp.float32)
    key_grad = (jnp.einsum('jgtu,tjgd->ujd', logit_low, query_heads) * scale).astype(jnp.bfloat16)
    onehot = (segment[:, None] == jnp.arange(EX_DEV, dtype=jnp.int32)[None, :]).astype(jnp.float32)
    return (key_grad.reshape(count, KVH * HD), value_grad.reshape(count, KVH * HD), onehot)

def one_block(inputs, norm_gain, value_weight, input_basis, output_basis):
    tokens, queries, keys, upstream, lengths = inputs
    activ = tokens.astype(jnp.float32)
    mean_square = lax.optimization_barrier(jnp.mean(activ * activ, axis=1, keepdims=True))
    normed = (activ * lax.rsqrt(mean_square + 1e-05) * norm_gain.astype(jnp.float32)).astype(jnp.bfloat16)
    values = jnp.dot(normed, value_weight, preferred_element_type=jnp.float32).astype(jnp.bfloat16)
    left = jnp.dot(normed, input_basis, preferred_element_type=jnp.float32)
    key_grad, value_grad, onehot = attend(queries, keys, values, upstream, lengths)
    right = jnp.dot(value_grad, output_basis, preferred_element_type=jnp.float32)
    per_example = jnp.einsum('te,ti,tj->eij', onehot, left, right, precision=lax.Precision.HIGHEST)
    return (key_grad, per_example.reshape(EX_DEV, RANK * RANK).astype(jnp.bfloat16))

def reference(tokens, norm_gain, value_weight, input_basis, output_basis, rotated_queries, rotated_keys, upstream_grad, example_lengths, query_grads):
    blocks = N_DP * N_FSDP
    inputs = (tokens.reshape(blocks, TOK_DEV, D), rotated_queries.reshape(blocks, TOK_DEV, KVH * GROUP * HD), rotated_keys.reshape(blocks, TOK_DEV, KVH * HD), upstream_grad.reshape(blocks, TOK_DEV, KVH * GROUP * HD), example_lengths)
    key_grad, train_grads = lax.map(partial_block(norm_gain, value_weight, input_basis, output_basis), inputs)
    influence = lax.dot_general(train_grads.reshape(blocks * EX_DEV, RANK * RANK), query_grads, (((1,), (1,)), ((), ())), preferred_element_type=jnp.float32)
    return (key_grad.reshape(blocks * TOK_DEV, KVH * HD), influence)

def partial_block(norm_gain, value_weight, input_basis, output_basis):

    def apply_block(inputs):
        return one_block(inputs, norm_gain, value_weight, input_basis, output_basis)
    return apply_block
```

```python
import math

import jax
import jax.numpy as jnp
from jax import lax
from jax.sharding import Mesh
from jax.sharding import PartitionSpec as P

HD = 128
GROUP = 8
KVH = 4
RANK = 64
LANES = 128

epsilon = 1e-05

AXES = ("zh", "x", "c", "y", "zl")
SIZES = (2, 4, 2, 4, 8)


def width(axes):
    return math.prod(lax.axis_size(a) for a in axes)


def exchange(blocks, axes):
    return lax.all_to_all(blocks, axes, 0, 0, tiled=False)


def spread(block, axes):
    return exchange(jnp.broadcast_to(block[None], (width(axes),) + block.shape), axes)


def segments(lengths, count):
    bounds = jnp.cumsum(lengths)
    places = jnp.arange(count, dtype=jnp.int32)
    return jnp.sum((places[:, None] >= bounds[None, :]).astype(jnp.int32), axis=1)


def attend(queries, keys, values, upstream, segment):
    count = queries.shape[0]
    places = jnp.arange(count, dtype=jnp.int32)
    query_heads = queries.reshape(count, KVH, GROUP, HD)
    key_heads = keys.reshape(count, KVH, HD)
    value_heads = values.reshape(count, KVH, HD)
    grad_heads = upstream.reshape(count, KVH, GROUP, HD)
    allowed = (segment[:, None] == segment[None, :]) & (places[None, :] <= places[:, None])
    scale = 1.0 / math.sqrt(HD)
    logits = (
        jnp.einsum("tjgd,ujd->jgtu", query_heads, key_heads, preferred_element_type=jnp.float32)
        * scale
    )
    logits = jnp.where(allowed, logits, jnp.float32(-1e30))
    row_max = jnp.max(logits, axis=-1, keepdims=True)
    expo = jnp.exp(logits - row_max)
    probs = expo / jnp.sum(expo, axis=-1, keepdims=True)
    probs_low = probs.astype(jnp.bfloat16)
    value_grad = jnp.einsum(
        "jgtu,tjgd->ujd", probs_low, grad_heads, preferred_element_type=jnp.float32
    ).astype(jnp.bfloat16)
    prob_grad = jnp.einsum(
        "tjgd,ujd->jgtu", grad_heads, value_heads, preferred_element_type=jnp.float32
    )
    logit_grad = probs * (prob_grad - jnp.sum(probs * prob_grad, axis=-1, keepdims=True))
    logit_low = logit_grad.astype(jnp.bfloat16)
    key_grad = (
        jnp.einsum("jgtu,tjgd->ujd", logit_low, query_heads, preferred_element_type=jnp.float32)
        * scale
    ).astype(jnp.bfloat16)
    return key_grad.reshape(count, KVH * HD), value_grad.reshape(count, KVH * HD)


def gather_weights(norm_gain, value_weight, input_basis):
    rows = value_weight.shape[0]
    half = rows // lax.axis_size("c")
    piece = half // lax.axis_size("x")
    shard = lax.axis_index("y") * lax.axis_size("zl") + lax.axis_index("zl")
    gain = lax.dynamic_slice_in_dim(norm_gain, shard * rows, rows, 0).astype(jnp.float32)
    both = jnp.concatenate([value_weight, input_basis], axis=1).astype(jnp.float32)
    both = (both * gain[:, None]).astype(jnp.bfloat16)
    begin = lax.axis_index("c") * half + lax.axis_index("x") * piece
    mine = lax.dynamic_slice_in_dim(both, begin, piece, 0)
    along_z = spread(mine, ("zl",))
    along_x = spread(along_z, ("x",))
    return along_x.transpose(1, 0, 2, 3).reshape(-1, both.shape[1])


def project(tokens, weights):
    count, features = tokens.shape
    cs, ys, zs = lax.axis_size("c"), lax.axis_size("y"), lax.axis_size("zl")
    piece = features // (cs * ys * zs)
    blocks = tokens.reshape(count, ys, zs, cs, piece).transpose(3, 1, 0, 2, 4)
    blocks = exchange(blocks.reshape(cs * ys, count, zs * piece), ("c", "y"))
    part = jnp.einsum("smk,kn->smn", blocks, weights, preferred_element_type=jnp.float32)
    wide = KVH * HD
    value_part, left_part = part[..., :wide], part[..., wide:]
    left_high = lax.reduce_precision(left_part, 8, 7)
    sent = jnp.concatenate([value_part, left_high, left_part - left_high], axis=2)
    came = exchange(sent.astype(jnp.bfloat16), ("c", "y")).astype(jnp.float32)
    total = jnp.sum(came, axis=0)
    return total[:, :wide], total[:, wide : wide + RANK] + total[:, wide + RANK :]


def gather_queries(query_grads):
    rows, length = query_grads.shape
    along_z = spread(query_grads, ("zh", "zl"))
    along_y = spread(along_z, ("y",))
    by_axis = along_y.reshape(
        lax.axis_size("y"), lax.axis_size("zh"), lax.axis_size("zl"), rows, length
    )
    return by_axis.transpose(1, 0, 2, 3, 4).reshape(-1, length)


def score(train_grads, some_queries):
    count = train_grads.shape[0]
    xs, cs, zhs = lax.axis_size("x"), lax.axis_size("c"), lax.axis_size("zh")
    others = spread(train_grads, ("x", "c")).reshape(xs * cs * count, -1)
    block = lax.dot_general(
        others, some_queries, (((1,), (1,)), ((), ())), preferred_element_type=jnp.float32
    )
    came = exchange(block.reshape(xs * cs, count, -1), ("x", "c"))
    came = came.reshape(xs, cs, count, zhs, -1)
    return came.transpose(2, 3, 0, 1, 4).reshape(count, -1)


def on_device(
    tokens,
    norm_gain,
    value_weight,
    input_basis,
    output_basis,
    rotated_queries,
    rotated_keys,
    upstream_grad,
    example_lengths,
    query_grads,
):
    some_queries = gather_queries(query_grads)
    weights = gather_weights(norm_gain, value_weight, input_basis)
    value_sum, left_sum = project(tokens, weights)
    activ = tokens.astype(jnp.float32)
    row_scale = lax.rsqrt(jnp.mean(activ * activ, axis=1, keepdims=True) + epsilon)
    values = (value_sum * row_scale).astype(jnp.bfloat16)
    left = left_sum * row_scale
    segment = segments(example_lengths[0], tokens.shape[0])
    key_grad, value_grad = attend(rotated_queries, rotated_keys, values, upstream_grad, segment)
    right = jnp.dot(value_grad, output_basis, preferred_element_type=jnp.float32)
    examples = example_lengths.shape[1]
    onehot = (segment[:, None] == jnp.arange(examples, dtype=jnp.int32)[None, :]).astype(jnp.float32)
    per_example = jnp.einsum("te,ti,tj->eij", onehot, left, right, precision=lax.Precision.HIGHEST)
    train_grads = per_example.reshape(examples, -1).astype(jnp.bfloat16)
    return (key_grad, score(train_grads, some_queries))


def solution(mesh):
    fine = Mesh(mesh.devices.reshape(SIZES), AXES)
    rows = P(AXES, None)
    return jax.shard_map(
        on_device,
        mesh=fine,
        in_specs=(
            rows,
            P(),
            P(("y", "zl"), None),
            P(("y", "zl"), None),
            P(),
            rows,
            rows,
            rows,
            rows,
            rows,
        ),
        out_specs=(rows, rows),
        check_vma=False,
    )
```

```python
import math

import jax
import jax.numpy as jnp
from jax import lax
from jax.experimental import pallas as pl
from jax.experimental.pallas import tpu as pltpu
from jax.sharding import Mesh
from jax.sharding import PartitionSpec as P

HD = 128
GROUP = 8
KVH = 4
RANK = 64
LANES = 128
QUERY_ROWS = 16

epsilon = 1e-05

AXES = ("zh", "x", "c", "y", "zl")
SIZES = (2, 4, 2, 4, 8)


def width(axes):
    return math.prod(lax.axis_size(a) for a in axes)


def exchange(blocks, axes):
    return lax.all_to_all(blocks, axes, 0, 0, tiled=False)


def spread(block, axes):
    return exchange(jnp.broadcast_to(block[None], (width(axes),) + block.shape), axes)


def segments(lengths, count):
    bounds = jnp.cumsum(lengths)
    places = jnp.arange(count, dtype=jnp.int32)
    return jnp.sum((places[:, None] >= bounds[None, :]).astype(jnp.int32), axis=1)


def attend_probs(queries, keys, upstream, segment):
    count = queries.shape[0]
    places = jnp.arange(count, dtype=jnp.int32)
    query_heads = queries.reshape(count, KVH, GROUP, HD)
    key_heads = keys.reshape(count, KVH, HD)
    grad_heads = upstream.reshape(count, KVH, GROUP, HD)
    allowed = (segment[:, None] == segment[None, :]) & (places[None, :] <= places[:, None])
    scale = 1.0 / math.sqrt(HD)
    logits = (
        jnp.einsum("tjgd,ujd->jgtu", query_heads, key_heads, preferred_element_type=jnp.float32)
        * scale
    )
    logits = jnp.where(allowed, logits, jnp.float32(-1e30))
    row_max = jnp.max(logits, axis=-1, keepdims=True)
    expo = jnp.exp(logits - row_max)
    probs = expo / jnp.sum(expo, axis=-1, keepdims=True)
    value_grad = jnp.einsum(
        "jgtu,tjgd->ujd",
        probs.astype(jnp.bfloat16),
        grad_heads,
        preferred_element_type=jnp.float32,
    ).astype(jnp.bfloat16)
    return probs, value_grad.reshape(count, KVH * HD)


def attend_keys(queries, probs, values, upstream):
    count = queries.shape[0]
    query_heads = queries.reshape(count, KVH, GROUP, HD)
    value_heads = values.reshape(count, KVH, HD)
    grad_heads = upstream.reshape(count, KVH, GROUP, HD)
    prob_grad = jnp.einsum(
        "tjgd,ujd->jgtu", grad_heads, value_heads, preferred_element_type=jnp.float32
    )
    logit_grad = probs * (prob_grad - jnp.sum(probs * prob_grad, axis=-1, keepdims=True))
    logit_low = logit_grad.astype(jnp.bfloat16)
    key_grad = jnp.einsum("jgtu,tjgd->ujd", logit_low, query_heads, preferred_element_type=jnp.float32)
    return (key_grad * (1.0 / math.sqrt(HD))).astype(jnp.bfloat16).reshape(count, KVH * HD)


def spec(space):
    return pl.BlockSpec(memory_space=space)


def local_kernel(body, out_shape, scratch=(), flops=0, moved=0):
    def call(place, *arrays):
        return pl.pallas_call(
            body,
            out_shape=out_shape,
            in_specs=[spec(pltpu.SMEM)] + [spec(pltpu.VMEM)] * len(arrays),
            out_specs=jax.tree.map(lambda _: spec(pltpu.VMEM), out_shape),
            scratch_shapes=scratch,
            compiler_params=pltpu.CompilerParams(vmem_limit_bytes=40 * 1024 * 1024),
            cost_estimate=pl.CostEstimate(flops=flops, bytes_accessed=moved, transcendentals=0),
        )(place, *arrays)

    return call


def scaled_weights_kernel(place, gain, values, basis, out, turned):
    c, x, block = place[0], place[1], place[2]
    rows = pl.ds(pl.multiple_of(c * LANES, LANES), LANES)
    mine = lax.broadcasted_iota(jnp.int32, gain.shape, 0) == block
    factor = jnp.sum(jnp.where(mine, gain[...].astype(jnp.float32), 0.0), axis=0, keepdims=True)
    head = values[rows, pl.ds(pl.multiple_of(x * HD, HD), HD)].astype(jnp.float32)
    turned[...] = basis[rows, :].astype(jnp.float32).T
    share = out.shape[1] - HD
    some = turned[pl.ds(pl.multiple_of(x * share, share), share), :]
    piece = jnp.concatenate([head.T, some], axis=0) * factor
    out[...] = jnp.broadcast_to(piece.astype(out.dtype)[None], out.shape)


def gather_weights(norm_gain, value_weight, input_basis):
    c, x = lax.axis_index("c"), lax.axis_index("x")
    zs = lax.axis_size("zl")
    shard = lax.axis_index("y") * zs + lax.axis_index("zl")
    place = jnp.stack([c, x, shard * lax.axis_size("c") + c]).astype(jnp.int32)
    share = RANK // lax.axis_size("x")
    sent = local_kernel(
        scaled_weights_kernel,
        jax.ShapeDtypeStruct((zs, HD + share, LANES), jnp.bfloat16),
        (pltpu.VMEM((RANK, LANES), jnp.float32),),
        moved=1 << 20,
    )(place, norm_gain.reshape(-1, LANES), value_weight, input_basis)
    return exchange(sent, ("zl",))


def swapped(block):
    return lax.ppermute(block, "c", [(0, 1), (1, 0)])


def share_tokens(tokens):
    ys = lax.axis_size("y")
    features = tokens.shape[1] // ys
    blocks = []
    for s in range(ys):
        target = lax.rem(lax.axis_index("y") + s, ys)
        block = lax.dynamic_slice_in_dim(tokens, target * features, features, 1)
        if s:
            block = lax.ppermute(block, "y", [(i, (i + s) % ys) for i in range(ys)])
        blocks.append(block)
    return blocks


def lay_out(weights, whole):
    xs, zs, width_, depth = weights.shape
    share = width_ - HD
    for x in range(xs):
        for z in range(zs):
            features = slice(z * depth, (z + 1) * depth)
            whole[x * HD : (x + 1) * HD, features] = weights[x, z, :HD, :]
            begin = xs * HD + x * share
            whole[begin : begin + share, features] = weights[x, z, HD:, :]


def half_product(half, weights, blocks, rows, whole):
    lay_out(weights, whole)
    count, depth = blocks[0].shape[0], weights.shape[3]
    for distance, block in enumerate(blocks):
        for z in range(weights.shape[1]):
            begin = pl.multiple_of((2 * z + half) * depth, depth)
            rows[distance * count : (distance + 1) * count, z * depth : (z + 1) * depth] = block[
                :, pl.ds(begin, depth)
            ]
    return lax.dot_general(
        rows[...], whole[...], (((1,), (1,)), ((), ())), preferred_element_type=jnp.float32
    )


def own_half_kernel(place, weights, *refs):
    *blocks, out, rows, whole = refs
    out[...] = half_product(place[1], weights, blocks, rows, whole)


def partner_half_kernel(place, weights, begun, *refs):
    *blocks, out, rows, whole = refs
    count, wide, ys = blocks[0].shape[0], KVH * HD, len(blocks)
    total = begun[...] + half_product(1 - place[1], weights, blocks, rows, whole)
    left = total[:, wide:]
    high = left.astype(jnp.bfloat16)
    low = (left - high.astype(jnp.float32)).astype(jnp.bfloat16)
    sent = jnp.concatenate([total[:, :wide].astype(jnp.bfloat16), high, low], axis=1)
    for distance in range(ys):
        out[lax.rem(place[0] - distance + ys, ys)] = sent[distance * count : (distance + 1) * count]


def project(blocks, weights):
    ys, count = len(blocks), blocks[0].shape[0]
    xs, zs, width_, depth = weights.shape
    columns = xs * width_
    place = jnp.stack([lax.axis_index("y"), lax.axis_index("c")]).astype(jnp.int32)
    scratch = (
        pltpu.VMEM((ys * count, zs * depth), jnp.bfloat16),
        pltpu.VMEM((columns, zs * depth), jnp.bfloat16),
    )
    cost = dict(flops=2 * ys * count * columns * zs * depth, moved=4 << 20)
    part = jax.ShapeDtypeStruct((ys * count, columns), jnp.float32)
    begun = local_kernel(own_half_kernel, part, scratch, **cost)(place, weights, *blocks)
    sent = jax.ShapeDtypeStruct((ys, count, columns + RANK), jnp.bfloat16)
    other = swapped(weights)
    return local_kernel(partner_half_kernel, sent, scratch, **cost)(place, other, begun, *blocks)


def spread_along_z(query_grads):
    rows = query_grads.shape[0]
    sent = jnp.pad(query_grads, ((0, QUERY_ROWS - rows), (0, 0)))
    return lax.all_gather(sent, ("zh", "zl"), axis=0, tiled=False)[:, :rows]


def spread_along_y(some_queries):
    ys = lax.axis_size("y")
    return jnp.concatenate(
        [some_queries]
        + [lax.ppermute(some_queries, "y", [(i, (i + s) % ys) for i in range(ys)]) for s in range(1, ys)],
        axis=0,
    )


def query_order(rows):
    zhs, ys, zs = (lax.axis_size(a) for a in ("zh", "y", "zl"))
    n = jnp.arange(zhs * ys * zs * rows, dtype=jnp.int32)
    row, zl, y, zh = n % rows, n // rows % zs, n // (rows * zs) % ys, n // (rows * zs * ys)
    distance = (lax.axis_index("y").astype(jnp.int32) - y) % ys
    k = ((distance * zhs + zh) * zs + zl) * rows + row
    return (n[:, None] == k[None, :]).astype(jnp.float32)


def score(others, some_queries, pick):
    xs, cs, zhs = lax.axis_size("x"), lax.axis_size("c"), lax.axis_size("zh")
    count = others.shape[1]
    block = lax.dot_general(
        others.reshape(xs * cs * count, -1),
        some_queries,
        (((1,), (1,)), ((), ())),
        preferred_element_type=jnp.float32,
    )
    block = jnp.dot(block, pick, precision=lax.Precision.HIGHEST)
    came = exchange(block.reshape(xs * cs, count, -1), ("x", "c"))
    came = came.reshape(xs, cs, count, zhs, -1)
    return came.transpose(2, 3, 0, 1, 4).reshape(count, -1)


def on_device(
    tokens,
    norm_gain,
    value_weight,
    input_basis,
    output_basis,
    rotated_queries,
    rotated_keys,
    upstream_grad,
    example_lengths,
    query_grads,
):
    some_queries = spread_along_z(query_grads)
    along_z = gather_weights(norm_gain, value_weight, input_basis)
    token_blocks = share_tokens(tokens)
    segment = segments(example_lengths[0], tokens.shape[0])
    probs, value_grad = attend_probs(rotated_queries, rotated_keys, upstream_grad, segment)
    right = jnp.dot(value_grad, output_basis, preferred_element_type=jnp.float32)
    along_z, right, token_blocks[1], token_blocks[-1] = lax.optimization_barrier(
        (along_z, right, token_blocks[1], token_blocks[-1])
    )

    weights = spread(along_z, ("x",))
    activ = tokens.astype(jnp.float32)
    row_scale = lax.rsqrt(jnp.mean(activ * activ, axis=1, keepdims=True) + epsilon)
    weights, row_scale, *token_blocks = lax.optimization_barrier((weights, row_scale, *token_blocks))

    came = exchange(project(token_blocks, weights), ("y",))
    pick = query_order(query_grads.shape[0])
    came, pick = lax.optimization_barrier((came, pick))
    total = jnp.sum(came.astype(jnp.float32), axis=0)
    wide = KVH * HD
    values = (total[:, :wide] * row_scale).astype(jnp.bfloat16)
    left = (total[:, wide : wide + RANK] + total[:, wide + RANK :]) * row_scale

    examples = example_lengths.shape[1]
    onehot = (segment[:, None] == jnp.arange(examples, dtype=jnp.int32)[None, :]).astype(jnp.float32)
    per_example = jnp.einsum("te,ti,tj->eij", onehot, left, right, precision=lax.Precision.HIGHEST)
    train_grads = per_example.reshape(examples, -1).astype(jnp.bfloat16)
    others = spread(train_grads, ("x", "c"))
    gathered = spread_along_y(some_queries.reshape(-1, some_queries.shape[-1]))
    key_grad = attend_keys(rotated_queries, probs, values, upstream_grad)
    others, gathered = lax.optimization_barrier((others, gathered))
    return (key_grad, score(others, gathered, pick))


def solution(mesh):
    fine = Mesh(mesh.devices.reshape(SIZES), AXES)
    rows = P(AXES, None)
    return jax.shard_map(
        on_device,
        mesh=fine,
        in_specs=(
            rows,
            P(),
            P(("y", "zl"), None),
            P(("y", "zl"), None),
            P(),
            rows,
            rows,
            rows,
            rows,
            rows,
        ),
        out_specs=(rows, rows),
        check_vma=False,
    )
```

```python
import itertools
import math

import jax
import jax.numpy as jnp
from jax import lax
from jax.experimental import pallas as pl
from jax.experimental.pallas import tpu as pltpu
from jax.sharding import Mesh
from jax.sharding import PartitionSpec as P

HD = 128
GROUP = 8
KVH = 4
RANK = 64
LANES = 128

epsilon = 1e-05

AXES = ("zh", "x", "c", "y", "zl")
SIZES = (2, 4, 2, 4, 8)
XS = 4


def width(axes):
    return math.prod(lax.axis_size(a) for a in axes)


def exchange(blocks, axes):
    return lax.all_to_all(blocks, axes, 0, 0, tiled=False)


def spread(block, axes):
    return exchange(jnp.broadcast_to(block[None], (width(axes),) + block.shape), axes)


def segments(lengths, count):
    bounds = jnp.cumsum(lengths)
    places = jnp.arange(count, dtype=jnp.int32)
    return jnp.sum((places[:, None] >= bounds[None, :]).astype(jnp.int32), axis=1)


def spec(space):
    return pl.BlockSpec(memory_space=space)


def local_kernel(body, out_shape, scratch=(), flops=0, moved=0):
    def call(place, *arrays):
        return pl.pallas_call(
            body,
            out_shape=out_shape,
            in_specs=[spec(pltpu.SMEM)] + [spec(pltpu.VMEM)] * len(arrays),
            out_specs=jax.tree.map(lambda _: spec(pltpu.VMEM), out_shape),
            scratch_shapes=scratch,
            compiler_params=pltpu.CompilerParams(vmem_limit_bytes=16 * 1024 * 1024),
            cost_estimate=pl.CostEstimate(flops=flops, bytes_accessed=moved, transcendentals=0),
        )(place, *arrays)

    return call


def segment_of(lengths, index):
    found, bound = jnp.zeros_like(index), 0
    for e in range(lengths.shape[1]):
        bound = bound + lengths[0, e]
        found = found + (index >= bound).astype(jnp.int32)
    return found


def group_rows(array, j):
    heads = [array[:, (j * GROUP + g) * HD : (j * GROUP + g + 1) * HD] for g in range(GROUP)]
    return jnp.concatenate(heads, axis=0)


def probs_kernel(lengths, queries, keys, upstream, basis, probs, right):
    count = queries.shape[0]
    row = lax.broadcasted_iota(jnp.int32, (count, count), 0)
    column = lax.broadcasted_iota(jnp.int32, (count, count), 1)
    allowed = (segment_of(lengths, row) == segment_of(lengths, column)) & (row <= column)
    fence = jnp.where(allowed, 0.0, -1e30).astype(jnp.float32)
    fence = jnp.concatenate([fence] * GROUP, axis=1)
    scale = 1.0 / math.sqrt(HD)
    grads = []
    for j in range(KVH):
        logits = lax.dot_general(
            keys[:, j * HD : (j + 1) * HD],
            group_rows(queries, j),
            (((1,), (1,)), ((), ())),
            preferred_element_type=jnp.float32,
        )
        logits = jnp.where(fence == 0.0, logits * scale, fence)
        expo = jnp.exp(logits - jnp.max(logits, axis=0, keepdims=True))
        prob = expo * (1.0 / jnp.sum(expo, axis=0, keepdims=True))
        probs[j] = prob
        grad = jnp.dot(
            prob.astype(jnp.bfloat16), group_rows(upstream, j), preferred_element_type=jnp.float32
        )
        grads.append(grad.astype(jnp.bfloat16))
    right[...] = lax.dot_general(
        jnp.concatenate(grads, axis=1),
        basis[...],
        (((1,), (1,)), ((), ())),
        preferred_element_type=jnp.float32,
    )


def keys_kernel(lengths, queries, probs, values, upstream, key_grad):
    scale = 1.0 / math.sqrt(HD)
    for j in range(KVH):
        columns = slice(j * HD, (j + 1) * HD)
        prob_grad = lax.dot_general(
            values[:, columns],
            group_rows(upstream, j),
            (((1,), (1,)), ((), ())),
            preferred_element_type=jnp.float32,
        )
        prob = probs[j]
        mean = jnp.sum(prob * prob_grad, axis=0, keepdims=True)
        logit_grad = (prob * (prob_grad - mean)).astype(jnp.bfloat16)
        grad = jnp.dot(logit_grad, group_rows(queries, j), preferred_element_type=jnp.float32)
        key_grad[:, columns] = (grad * scale).astype(jnp.bfloat16)


def attend_probs(queries, keys, upstream, lengths, basis):
    count = queries.shape[0]
    out = (
        jax.ShapeDtypeStruct((KVH, count, GROUP * count), jnp.float32),
        jax.ShapeDtypeStruct((count, RANK), jnp.float32),
    )
    cost = dict(flops=4 * KVH * GROUP * count * count * HD, moved=5 << 20)
    return local_kernel(probs_kernel, out, **cost)(lengths, queries, keys, upstream, basis.T)


def attend_keys(queries, probs, values, upstream, lengths):
    out = jax.ShapeDtypeStruct(values.shape, jnp.bfloat16)
    cost = dict(flops=4 * KVH * GROUP * HD * values.shape[0] ** 2, moved=5 << 20)
    return local_kernel(keys_kernel, out, **cost)(lengths, queries, probs, values, upstream)


def first_kernel(place, gain, values, basis, queries, out, turned):
    c, x, block = place[0], place[1], place[2]
    rows = pl.ds(pl.multiple_of(c * LANES, LANES), LANES)
    mine = lax.broadcasted_iota(jnp.int32, gain.shape, 0) == block
    factor = jnp.sum(jnp.where(mine, gain[...].astype(jnp.float32), 0.0), axis=0, keepdims=True)
    head = values[rows, pl.ds(pl.multiple_of(x * HD, HD), HD)].astype(jnp.float32)
    turned[...] = basis[:, rows].astype(jnp.float32)
    share = RANK // XS
    some = turned[pl.ds(pl.multiple_of(x * share, share), share), :]
    piece = jnp.concatenate([head.T, some], axis=0) * factor
    length = queries.shape[1] // LANES
    wide = queries[...].astype(jnp.float32)
    cut = [wide[:, k * LANES : (k + 1) * LANES] for k in range(length)]
    both = jnp.concatenate([piece] + cut, axis=0).astype(out.dtype)
    out[...] = jnp.broadcast_to(both[None], out.shape)


def gather_along_z(norm_gain, value_weight, input_basis, query_grads):
    c, x = lax.axis_index("c"), lax.axis_index("x")
    zs = lax.axis_size("zl")
    shard = lax.axis_index("y") * zs + lax.axis_index("zl")
    place = jnp.stack([c, x, shard * lax.axis_size("c") + c]).astype(jnp.int32)
    columns = HD + RANK // lax.axis_size("x")
    rows, length = query_grads.shape
    sent = local_kernel(
        first_kernel,
        jax.ShapeDtypeStruct((zs, columns + rows * length // LANES, LANES), jnp.bfloat16),
        (pltpu.VMEM((RANK, LANES), jnp.float32),),
        moved=1 << 20,
    )(place, norm_gain.reshape(-1, LANES), value_weight, input_basis.T, query_grads)
    came = exchange(sent, ("zl",))
    queries = came[:, columns:].reshape(zs, length // LANES, rows, LANES)
    return came[:, :columns], queries.transpose(0, 2, 1, 3).reshape(zs * rows, length)


def swapped(block):
    return lax.ppermute(block, "c", [(0, 1), (1, 0)])


def share_tokens(tokens):
    ys = lax.axis_size("y")
    features = tokens.shape[1] // ys
    blocks = []
    for s in range(ys):
        target = lax.rem(lax.axis_index("y") + s, ys)
        block = lax.dynamic_slice_in_dim(tokens, target * features, features, 1)
        if s:
            block = lax.ppermute(block, "y", [(i, (i + s) % ys) for i in range(ys)])
        blocks.append(block)
    return blocks


def lay_out(weights, half, whole):
    xs, zs, width_, depth = weights.shape
    share = width_ - HD
    for z in range(zs):
        features = pl.ds(pl.multiple_of((2 * z + half) * depth, depth), depth)
        for x in range(xs):
            whole[x * HD : (x + 1) * HD, features] = weights[x, z, :HD, :]
            begin = xs * HD + x * share
            whole[begin : begin + share, features] = weights[x, z, HD:, :]


def product_kernel(place, own, partners, *refs):
    *blocks, out, whole = refs
    y, c = place[0], place[1]
    count, wide, ys = blocks[0].shape[0], KVH * HD, len(blocks)
    lay_out(own, c, whole)
    lay_out(partners, 1 - c, whole)
    total = lax.dot_general(
        jnp.concatenate([block[...] for block in blocks], axis=0),
        whole[...],
        (((1,), (1,)), ((), ())),
        preferred_element_type=jnp.float32,
    )
    left = total[:, wide:]
    high = left.astype(jnp.bfloat16)
    low = (left - high.astype(jnp.float32)).astype(jnp.bfloat16)
    sent = jnp.concatenate([total[:, :wide].astype(jnp.bfloat16), high, low], axis=1)
    for distance in range(ys):
        out[lax.rem(y - distance + ys, ys)] = sent[distance * count : (distance + 1) * count]


def project(blocks, weights):
    ys, (count, features) = len(blocks), blocks[0].shape
    xs, _, width_, _ = weights.shape
    columns = xs * width_
    place = jnp.stack([lax.axis_index("y"), lax.axis_index("c")]).astype(jnp.int32)
    return local_kernel(
        product_kernel,
        jax.ShapeDtypeStruct((ys, count, columns + RANK), jnp.bfloat16),
        (pltpu.VMEM((columns, features), jnp.bfloat16),),
        flops=2 * ys * count * columns * features,
        moved=6 << 20,
    )(place, weights, swapped(weights), *blocks)


def pair(block, axis, bit):
    size = lax.axis_size(axis)
    other = lax.ppermute(block, axis, [(i, i ^ bit) for i in range(size)])
    return jnp.concatenate([block, other], axis=0)


def bits(axis):
    return [1 << k for k in range(lax.axis_size(axis).bit_length() - 1)]


def query_steps():
    return [("zh", b) for b in bits("zh")] + [("y", b) for b in bits("y")]


def query_order(rows):
    sizes = [lax.axis_size(a) for a in ("zh", "y", "zl")]
    n = jnp.arange(math.prod(sizes) * rows, dtype=jnp.int32)
    left, row = n // rows, n % rows
    where = {}
    for axis, size in zip(("zl", "y", "zh"), sizes[::-1]):
        where[axis] = left % size
        left = left // size
    k, weight = where["zl"] * rows + row, rows * sizes[2]
    for axis in ("y", "zh"):
        where[axis] = where[axis] ^ lax.axis_index(axis).astype(jnp.int32)
    for axis, bit in query_steps():
        k = k + jnp.where((where[axis] & bit) != 0, weight, 0)
        weight = weight * 2
    return (n[:, None] == k[None, :]).astype(jnp.float32)


def score(others, some_queries, pick):
    xs, cs, zhs = lax.axis_size("x"), lax.axis_size("c"), lax.axis_size("zh")
    count = others.shape[1]
    block = lax.dot_general(
        others.reshape(xs * cs * count, -1),
        some_queries,
        (((1,), (1,)), ((), ())),
        preferred_element_type=jnp.float32,
    )
    block = jnp.dot(block, pick, precision=lax.Precision.HIGHEST)
    came = exchange(block.reshape(xs * cs, count, -1), ("x", "c"))
    came = came.reshape(xs, cs, count, zhs, -1)
    return came.transpose(2, 3, 0, 1, 4).reshape(count, -1)


def on_device(
    tokens,
    norm_gain,
    value_weight,
    input_basis,
    output_basis,
    rotated_queries,
    rotated_keys,
    upstream_grad,
    example_lengths,
    query_grads,
):
    steps = iter(query_steps())
    along_z, gathered = gather_along_z(norm_gain, value_weight, input_basis, query_grads)
    blocks = share_tokens(tokens)
    along_z, gathered, blocks[1], blocks[-1] = lax.optimization_barrier(
        (along_z, gathered, blocks[1], blocks[-1])
    )

    weights = spread(along_z, ("x",))
    for step in itertools.islice(steps, 1):
        gathered = pair(gathered, *step)
    activ = tokens.astype(jnp.float32)
    row_scale = lax.rsqrt(jnp.mean(activ * activ, axis=1, keepdims=True) + epsilon)
    weights, gathered, *blocks = lax.optimization_barrier((weights, gathered, *blocks))

    sent = project(blocks, weights)
    sent, rotated_queries, upstream_grad = lax.optimization_barrier(
        (sent, rotated_queries, upstream_grad)
    )
    came = exchange(sent, ("y",))
    probs, right = attend_probs(
        rotated_queries, rotated_keys, upstream_grad, example_lengths, output_basis
    )
    for step in itertools.islice(steps, 1):
        gathered = pair(gathered, *step)
    pick = query_order(query_grads.shape[0])
    came, gathered, pick, right, row_scale = lax.optimization_barrier(
        (came, gathered, pick, right, row_scale)
    )
    total = jnp.sum(came.astype(jnp.float32), axis=0)
    wide = KVH * HD
    values = (total[:, :wide] * row_scale).astype(jnp.bfloat16)
    left = (total[:, wide : wide + RANK] + total[:, wide + RANK :]) * row_scale

    examples = example_lengths.shape[1]
    segment = segments(example_lengths[0], tokens.shape[0])
    onehot = (segment[:, None] == jnp.arange(examples, dtype=jnp.int32)[None, :]).astype(jnp.float32)
    per_example = jnp.einsum("te,ti,tj->eij", onehot, left, right, precision=lax.Precision.HIGHEST)
    train_grads = per_example.reshape(examples, -1).astype(jnp.bfloat16)
    others = spread(train_grads, ("x", "c"))
    for step in steps:
        gathered = pair(gathered, *step)
    key_grad = attend_keys(rotated_queries, probs, values, upstream_grad, example_lengths)
    others, gathered, key_grad = lax.optimization_barrier((others, gathered, key_grad))
    return (key_grad, score(others, gathered, pick))


def solution(mesh):
    fine = Mesh(mesh.devices.reshape(SIZES), AXES)
    rows = P(AXES, None)
    return jax.shard_map(
        on_device,
        mesh=fine,
        in_specs=(
            rows,
            P(),
            P(("y", "zl"), None),
            P(("y", "zl"), None),
            P(),
            rows,
            rows,
            rows,
            rows,
            rows,
        ),
        out_specs=(rows, rows),
        check_vma=False,
    )
```

```python
import itertools
import math

import jax
import jax.numpy as jnp
from jax import lax
from jax.experimental import pallas as pl
from jax.experimental.pallas import tpu as pltpu
from jax.sharding import Mesh
from jax.sharding import PartitionSpec as P

HD = 128
GROUP = 8
KVH = 4
RANK = 64
LANES = 128

epsilon = 1e-05

AXES = ("zh", "x", "c", "y", "zl")
SIZES = (2, 4, 2, 4, 8)
XS = 4


def width(axes):
    return math.prod(lax.axis_size(a) for a in axes)


def exchange(blocks, axes, groups=None):
    return lax.all_to_all(blocks, axes, 0, 0, axis_index_groups=groups, tiled=False)


def z_groups():
    zhs, zs = lax.axis_size("zh"), lax.axis_size("zl")
    return [[(h ^ (zl & 1)) * zs + zl for zl in range(zs)] for h in range(zhs)]


def spread(block, axes):
    return exchange(jnp.broadcast_to(block[None], (width(axes),) + block.shape), axes)


def segments(lengths, count):
    bounds = jnp.cumsum(lengths)
    places = jnp.arange(count, dtype=jnp.int32)
    return jnp.sum((places[:, None] >= bounds[None, :]).astype(jnp.int32), axis=1)


def spec(space):
    return pl.BlockSpec(memory_space=space)


def local_kernel(body, out_shape, scratch=(), flops=0, moved=0):
    def call(place, *arrays):
        return pl.pallas_call(
            body,
            out_shape=out_shape,
            in_specs=[spec(pltpu.SMEM)] + [spec(pltpu.VMEM)] * len(arrays),
            out_specs=jax.tree.map(lambda _: spec(pltpu.VMEM), out_shape),
            scratch_shapes=scratch,
            compiler_params=pltpu.CompilerParams(vmem_limit_bytes=16 * 1024 * 1024),
            cost_estimate=pl.CostEstimate(flops=flops, bytes_accessed=moved, transcendentals=0),
        )(place, *arrays)

    return call


def segment_of(lengths, index):
    found, bound = jnp.zeros_like(index), 0
    for e in range(lengths.shape[1]):
        bound = bound + lengths[0, e]
        found = found + (index >= bound).astype(jnp.int32)
    return found


def group_rows(array, j):
    heads = [array[:, (j * GROUP + g) * HD : (j * GROUP + g + 1) * HD] for g in range(GROUP)]
    return jnp.concatenate(heads, axis=0)


def probs_kernel(lengths, queries, keys, upstream, basis, probs, right):
    count = queries.shape[0]
    row = lax.broadcasted_iota(jnp.int32, (count, count), 0)
    column = lax.broadcasted_iota(jnp.int32, (count, count), 1)
    allowed = (segment_of(lengths, row) == segment_of(lengths, column)) & (row <= column)
    fence = jnp.where(allowed, 0.0, -1e30).astype(jnp.float32)
    fence = jnp.concatenate([fence] * GROUP, axis=1)
    scale = 1.0 / math.sqrt(HD)
    grads = []
    for j in range(KVH):
        logits = lax.dot_general(
            keys[:, j * HD : (j + 1) * HD],
            group_rows(queries, j),
            (((1,), (1,)), ((), ())),
            preferred_element_type=jnp.float32,
        )
        logits = jnp.where(fence == 0.0, logits * scale, fence)
        expo = jnp.exp(logits - jnp.max(logits, axis=0, keepdims=True))
        prob = expo * (1.0 / jnp.sum(expo, axis=0, keepdims=True))
        probs[j] = prob
        grad = jnp.dot(
            prob.astype(jnp.bfloat16), group_rows(upstream, j), preferred_element_type=jnp.float32
        )
        grads.append(grad.astype(jnp.bfloat16))
    right[...] = lax.dot_general(
        jnp.concatenate(grads, axis=1),
        basis[...],
        (((1,), (1,)), ((), ())),
        preferred_element_type=jnp.float32,
    )


def keys_kernel(lengths, queries, probs, values, upstream, key_grad):
    scale = 1.0 / math.sqrt(HD)
    for j in range(KVH):
        columns = slice(j * HD, (j + 1) * HD)
        prob_grad = lax.dot_general(
            values[:, columns],
            group_rows(upstream, j),
            (((1,), (1,)), ((), ())),
            preferred_element_type=jnp.float32,
        )
        prob = probs[j]
        mean = jnp.sum(prob * prob_grad, axis=0, keepdims=True)
        logit_grad = (prob * (prob_grad - mean)).astype(jnp.bfloat16)
        grad = jnp.dot(logit_grad, group_rows(queries, j), preferred_element_type=jnp.float32)
        key_grad[:, columns] = (grad * scale).astype(jnp.bfloat16)


def attend_probs(queries, keys, upstream, lengths, basis):
    count = queries.shape[0]
    out = (
        jax.ShapeDtypeStruct((KVH, count, GROUP * count), jnp.float32),
        jax.ShapeDtypeStruct((count, RANK), jnp.float32),
    )
    cost = dict(flops=4 * KVH * GROUP * count * count * HD, moved=5 << 20)
    return local_kernel(probs_kernel, out, **cost)(lengths, queries, keys, upstream, basis.T)


def attend_keys(queries, probs, values, upstream, lengths):
    out = jax.ShapeDtypeStruct(values.shape, jnp.bfloat16)
    cost = dict(flops=4 * KVH * GROUP * HD * values.shape[0] ** 2, moved=5 << 20)
    return local_kernel(keys_kernel, out, **cost)(lengths, queries, probs, values, upstream)


def first_kernel(place, gain, values, basis, queries, out, turned):
    c, x, block = place[0], place[1], place[2]
    rows = pl.ds(pl.multiple_of(c * LANES, LANES), LANES)
    mine = lax.broadcasted_iota(jnp.int32, gain.shape, 0) == block
    factor = jnp.sum(jnp.where(mine, gain[...].astype(jnp.float32), 0.0), axis=0, keepdims=True)
    head = values[rows, pl.ds(pl.multiple_of(x * HD, HD), HD)].astype(jnp.float32)
    turned[...] = basis[:, rows].astype(jnp.float32)
    share = RANK // XS
    some = turned[pl.ds(pl.multiple_of(x * share, share), share), :]
    piece = jnp.concatenate([head.T, some], axis=0) * factor
    length = queries.shape[1] // LANES
    wide = queries[...].astype(jnp.float32)
    cut = [wide[:, k * LANES : (k + 1) * LANES] for k in range(length)]
    both = jnp.concatenate([piece] + cut, axis=0).astype(out.dtype)
    out[...] = jnp.broadcast_to(both[None], out.shape)


def gather_along_z(norm_gain, value_weight, input_basis, query_grads):
    c, x = lax.axis_index("c"), lax.axis_index("x")
    zs = lax.axis_size("zl")
    shard = lax.axis_index("y") * zs + lax.axis_index("zl")
    place = jnp.stack([c, x, shard * lax.axis_size("c") + c]).astype(jnp.int32)
    columns = HD + RANK // lax.axis_size("x")
    rows, length = query_grads.shape
    sent = local_kernel(
        first_kernel,
        jax.ShapeDtypeStruct((zs, columns + rows * length // LANES, LANES), jnp.bfloat16),
        (pltpu.VMEM((RANK, LANES), jnp.float32),),
        moved=1 << 20,
    )(place, norm_gain.reshape(-1, LANES), value_weight, input_basis.T, query_grads)
    came = exchange(sent, ("zh", "zl"), z_groups())
    queries = came[:, columns:].reshape(zs, length // LANES, rows, LANES)
    return came[:, :columns], queries.transpose(0, 2, 1, 3).reshape(zs * rows, length)


def swapped(block):
    return lax.ppermute(block, "c", [(0, 1), (1, 0)])


def share_tokens(tokens):
    ys = lax.axis_size("y")
    features = tokens.shape[1] // ys
    blocks = []
    for s in range(ys):
        target = lax.rem(lax.axis_index("y") + s, ys)
        block = lax.dynamic_slice_in_dim(tokens, target * features, features, 1)
        if s:
            block = lax.ppermute(block, "y", [(i, (i + s) % ys) for i in range(ys)])
        blocks.append(block)
    return blocks


def lay_out(weights, half, whole):
    xs, zs, width_, depth = weights.shape
    share = width_ - HD
    for z in range(zs):
        features = pl.ds(pl.multiple_of((2 * z + half) * depth, depth), depth)
        for x in range(xs):
            whole[x * HD : (x + 1) * HD, features] = weights[x, z, :HD, :]
            begin = xs * HD + x * share
            whole[begin : begin + share, features] = weights[x, z, HD:, :]


def product_kernel(place, own, partners, *refs):
    *blocks, out, whole = refs
    y, c = place[0], place[1]
    count, wide, ys = blocks[0].shape[0], KVH * HD, len(blocks)
    lay_out(own, c, whole)
    lay_out(partners, 1 - c, whole)
    total = lax.dot_general(
        jnp.concatenate([block[...] for block in blocks], axis=0),
        whole[...],
        (((1,), (1,)), ((), ())),
        preferred_element_type=jnp.float32,
    )
    left = total[:, wide:]
    high = left.astype(jnp.bfloat16)
    low = (left - high.astype(jnp.float32)).astype(jnp.bfloat16)
    sent = jnp.concatenate([total[:, :wide].astype(jnp.bfloat16), high, low], axis=1)
    for distance in range(ys):
        out[lax.rem(y - distance + ys, ys)] = sent[distance * count : (distance + 1) * count]


def project(blocks, weights):
    ys, (count, features) = len(blocks), blocks[0].shape
    xs, _, width_, _ = weights.shape
    columns = xs * width_
    place = jnp.stack([lax.axis_index("y"), lax.axis_index("c")]).astype(jnp.int32)
    return local_kernel(
        product_kernel,
        jax.ShapeDtypeStruct((ys, count, columns + RANK), jnp.bfloat16),
        (pltpu.VMEM((columns, features), jnp.bfloat16),),
        flops=2 * ys * count * columns * features,
        moved=6 << 20,
    )(place, weights, swapped(weights), *blocks)


def pair(block, axis, bit):
    size = lax.axis_size(axis)
    other = lax.ppermute(block, axis, [(i, i ^ bit) for i in range(size)])
    return jnp.concatenate([block, other], axis=0)


def bits(axis):
    return [1 << k for k in range(lax.axis_size(axis).bit_length() - 1)]


def query_steps():
    return [("zl", 1)] + [("y", b) for b in bits("y")]


def query_order(rows):
    sizes = [lax.axis_size(a) for a in ("zh", "y", "zl")]
    n = jnp.arange(math.prod(sizes) * rows, dtype=jnp.int32)
    left, row = n // rows, n % rows
    where = {}
    for axis, size in zip(("zl", "y", "zh"), sizes[::-1]):
        where[axis] = left % size
        left = left // size
    k, weight = where["zl"] * rows + row, rows * sizes[2]
    group = where["zh"] ^ (where["zl"] & 1)
    own = lax.axis_index("zh") ^ (lax.axis_index("zl") & 1)
    k = k + (group ^ own.astype(jnp.int32)) * weight
    distance = where["y"] ^ lax.axis_index("y").astype(jnp.int32)
    k = k + distance * (weight * sizes[0])
    return (n[:, None] == k[None, :]).astype(jnp.float32)


def score(others, some_queries, pick):
    xs, cs, zhs = lax.axis_size("x"), lax.axis_size("c"), lax.axis_size("zh")
    count = others.shape[1]
    block = lax.dot_general(
        others.reshape(xs * cs * count, -1),
        some_queries,
        (((1,), (1,)), ((), ())),
        preferred_element_type=jnp.float32,
    )
    block = jnp.dot(block, pick, precision=lax.Precision.HIGHEST)
    came = exchange(block.reshape(xs * cs, count, -1), ("x", "c"))
    came = came.reshape(xs, cs, count, zhs, -1)
    return came.transpose(2, 3, 0, 1, 4).reshape(count, -1)


def on_device(
    tokens,
    norm_gain,
    value_weight,
    input_basis,
    output_basis,
    rotated_queries,
    rotated_keys,
    upstream_grad,
    example_lengths,
    query_grads,
):
    steps = iter(query_steps())
    along_z, gathered = gather_along_z(norm_gain, value_weight, input_basis, query_grads)
    blocks = share_tokens(tokens)
    along_z, gathered, blocks[1], blocks[-1] = lax.optimization_barrier(
        (along_z, gathered, blocks[1], blocks[-1])
    )

    weights = spread(along_z, ("x",))
    for step in itertools.islice(steps, 1):
        gathered = pair(gathered, *step)
    weights, gathered, *blocks = lax.optimization_barrier((weights, gathered, *blocks))

    sent = project(blocks, weights)
    sent, rotated_queries, upstream_grad, tokens = lax.optimization_barrier(
        (sent, rotated_queries, upstream_grad, tokens)
    )
    activ = tokens.astype(jnp.float32)
    row_scale = lax.rsqrt(jnp.mean(activ * activ, axis=1, keepdims=True) + epsilon)
    came = exchange(sent, ("y",))
    probs, right = attend_probs(
        rotated_queries, rotated_keys, upstream_grad, example_lengths, output_basis
    )
    for step in itertools.islice(steps, 1):
        gathered = pair(gathered, *step)
    pick = query_order(query_grads.shape[0])
    came, gathered, pick, right, row_scale = lax.optimization_barrier(
        (came, gathered, pick, right, row_scale)
    )
    total = jnp.sum(came.astype(jnp.float32), axis=0)
    wide = KVH * HD
    values = (total[:, :wide] * row_scale).astype(jnp.bfloat16)
    left = (total[:, wide : wide + RANK] + total[:, wide + RANK :]) * row_scale

    examples = example_lengths.shape[1]
    segment = segments(example_lengths[0], tokens.shape[0])
    onehot = (segment[:, None] == jnp.arange(examples, dtype=jnp.int32)[None, :]).astype(jnp.float32)
    per_example = jnp.einsum("te,ti,tj->eij", onehot, left, right, precision=lax.Precision.HIGHEST)
    train_grads = per_example.reshape(examples, -1).astype(jnp.bfloat16)
    others = spread(train_grads, ("x", "c"))
    for step in steps:
        gathered = pair(gathered, *step)
    key_grad = attend_keys(rotated_queries, probs, values, upstream_grad, example_lengths)
    others, gathered, key_grad = lax.optimization_barrier((others, gathered, key_grad))
    return (key_grad, score(others, gathered, pick))


def solution(mesh):
    fine = Mesh(mesh.devices.reshape(SIZES), AXES)
    rows = P(AXES, None)
    return jax.shard_map(
        on_device,
        mesh=fine,
        in_specs=(
            rows,
            P(),
            P(("y", "zl"), None),
            P(("y", "zl"), None),
            P(),
            rows,
            rows,
            rows,
            rows,
            rows,
        ),
        out_specs=(rows, rows),
        check_vma=False,
    )
```
